256 devices in a mesh: range: 4 (over x), depth: 64 (over y, z, core).
Axes of the slice: x: 4, y: 4, z: 8, core: 2. Of those that a mesh axis runs over, the one named last changes fastest.
Arguments:
- transfer_down: bfloat16 [2, 2, 4096, 4096], P(None, None, 'depth'), may hold values from -0.0625 to 0.0625
- transfer_up: bfloat16 [2, 2, 4096, 4096], P(None, None, 'depth'), may hold values from -0.0625 to 0.0625
- field_from_top: bfloat16 [2, 2, 4096, 4096], P(None, None, 'depth'), may hold values from -0.0625 to 0.0625
- field_from_bottom: bfloat16 [2, 2, 4096, 4096], P(None, None, 'depth'), may hold values from -0.0625 to 0.0625
- source_to_bottom: bfloat16 [2, 2, 4096, 4096], P(None, None, 'depth'), may hold values from -6 to 6
- source_to_top: bfloat16 [2, 2, 4096, 4096], P(None, None, 'depth'), may hold values from -6 to 6
- profile: int32 [4], P('range'), may hold values from 0 to 1
- source_depth: int32 [256], replicated, may hold values from 0 to 4095
Outputs:
- down_traces: bfloat16 [4, 2, 4096, 256], P('range', None, 'depth')
- up_traces: bfloat16 [4, 2, 4096, 256], P('range', None, 'depth')
- midline_field: float32 [4, 2, 4096, 256], P('range', None, 'depth')
The draws below stay inside these ranges and needn't reach their ends.
All inputs are finite; a program needn't handle non-finite values.
Results may differ from the reference program's by a relative error of at most 0.0033.
Values may be sent and summed in bfloat16 or wider, within the bound.
A program may use at most 128 MiB of HBM per device.

```python
import jax
import jax.numpy as jnp

M = 4096
SOURCES = 256
PROFILES = 2
LAYERS = 4


def touch_ends(entries, own_key, smallest, top_value):
    place = [jax.random.randint(jax.random.fold_in(own_key, axis), (), 0, length) for axis, length in enumerate(entries.shape)]
    widest = entries.shape.index(max(entries.shape))
    neighbour = place[:widest] + [(place[widest] + 1) % entries.shape[widest]] + place[widest + 1:]
    return entries.at[tuple(place)].set(smallest).at[tuple(neighbour)].set(top_value)


def level_of(stream_key, extent, cuts, least, high):
    loudness, own = 1.0, jax.random.fold_in(stream_key, 6)
    for dim, blocks in cuts:
        draws = jnp.exp(jax.random.uniform(jax.random.fold_in(own, dim), (blocks,), jnp.float32, least / len(cuts), high / len(cuts)))
        loudness = loudness * jnp.repeat(draws, extent[dim] // blocks).reshape([-1 if axis == dim else 1 for axis in range(len(extent))])
    return loudness


def gaussian(rng, dims, width, bound, cuts=(), held_as=jnp.bfloat16):
    level = level_of(rng, dims, cuts, -0.22, 0.18) if cuts else 1.0
    result = jax.random.normal(rng, dims, jnp.float32) * width * level
    return jnp.minimum(jnp.maximum(result, -bound), bound).astype(held_as)


def setup_inputs(seed: int = 0) -> dict:
    splits = jax.random.split(jax.random.key(seed), 9)
    transfer_down = gaussian(splits[0], (PROFILES, 2, M, M), (2 * M) ** -0.5, 0.0625, ((2, 64),))
    transfer_up = gaussian(splits[1], (PROFILES, 2, M, M), (2 * M) ** -0.5, 0.0625, ((2, 64),))
    field_from_top = gaussian(splits[2], (PROFILES, 2, M, M), (2 * M) ** -0.5, 0.0625, ((2, 64),))
    field_from_bottom = gaussian(splits[3], (PROFILES, 2, M, M), (2 * M) ** -0.5, 0.0625, ((2, 64),))
    source_to_bottom = gaussian(splits[4], (PROFILES, 2, M, M), 1.0, 6.0, ((2, 64),))
    source_to_top = gaussian(splits[5], (PROFILES, 2, M, M), 1.0, 6.0, ((2, 64),))
    profile = touch_ends(jax.random.randint(splits[6], (LAYERS,), 0, PROFILES), jax.random.fold_in(splits[6], 1), 0, PROFILES - 1).astype(jnp.int32)
    source_depth = touch_ends(jax.random.randint(splits[7], (SOURCES,), 0, M), jax.random.fold_in(splits[7], 1), 0, M - 1).astype(jnp.int32)
    return dict(transfer_down=transfer_down, transfer_up=transfer_up, field_from_top=field_from_top, field_from_bottom=field_from_bottom, source_to_bottom=source_to_bottom, source_to_top=source_to_top, profile=profile, source_depth=source_depth)


def complex_apply(matrix, trace):
    real_part = jnp.dot(matrix[0], trace[0], preferred_element_type=jnp.float32) - jnp.dot(matrix[1], trace[1], preferred_element_type=jnp.float32)
    imag_part = jnp.dot(matrix[0], trace[1], preferred_element_type=jnp.float32) + jnp.dot(matrix[1], trace[0], preferred_element_type=jnp.float32)
    return jnp.stack([real_part, imag_part])


def forcing(source_matrix, profile_index, layer_index, source_depth):
    columns = jnp.take(source_matrix[profile_index], source_depth, axis=2)
    active = (jnp.arange(SOURCES) % LAYERS) == layer_index
    return jnp.where(active[None, None, :], columns, jnp.zeros_like(columns))


def reference(transfer_down, transfer_up, field_from_top, field_from_bottom, source_to_bottom, source_to_top, profile, source_depth):
    downward = []
    for layer_index in range(LAYERS):
        profile_index = profile[layer_index]
        force_down = forcing(source_to_bottom, profile_index, layer_index, source_depth)
        if layer_index == 0:
            previous = force_down
        else:
            previous = (force_down.astype(jnp.float32) + complex_apply(transfer_down[profile_index], previous)).astype(jnp.bfloat16)
        downward.append(previous)
    upward = list(range(LAYERS))
    for layer_index in range(LAYERS - 1, -1, -1):
        profile_index = profile[layer_index]
        force_up = forcing(source_to_top, profile_index, layer_index, source_depth)
        if layer_index == LAYERS - 1:
            previous = force_up
        else:
            previous = (force_up.astype(jnp.float32) + complex_apply(transfer_up[profile_index], previous)).astype(jnp.bfloat16)
        upward[layer_index] = previous
    fields = []
    for layer_index in range(LAYERS):
        profile_index = profile[layer_index]
        field_part = jnp.zeros((2, M, SOURCES), jnp.float32)
        if layer_index > 0:
            field_part = complex_apply(field_from_top[profile_index], downward[layer_index - 1])
        if layer_index < LAYERS - 1:
            field_part = field_part + complex_apply(field_from_bottom[profile_index], upward[layer_index + 1])
        fields.append(field_part)
    return jnp.stack(downward), jnp.stack(upward), jnp.stack(fields)
```

```python
import functools

import jax
import jax.numpy as jnp
from jax import lax
from jax.experimental import pallas as pl
from jax.experimental.pallas import tpu as pltpu
from jax.sharding import PartitionSpec as P

MESH = pl.DeviceIdType.MESH
Y, Z, CORES = 4, 8, 2
PART = 32
DZ = (4, 3, -3, 2, -2, 1, -1)
DY = (2, 1, -1)
NEAR_Z = (5, 6, 3, 4, 1, 2, 0)
NEAR_Y = (1, 2, 0)
BF16, F32 = jnp.bfloat16, jnp.float32


def wait_bytes(ref, sem):
    pltpu.make_async_copy(ref, ref, sem).wait()


def rotate_parts(product):
    rows, columns = product.shape[0] // 2, product.shape[1]
    swapped = pltpu.roll(product[rows:], columns // 2, 1)
    lane = lax.broadcasted_iota(jnp.int32, swapped.shape, 1)
    return product[:rows] + jnp.where(lane < columns // 2, -swapped, swapped)


def kernel(
    profile, depth, t_down, t_up, f_top, f_bottom, s_bottom, s_top,
    down_out, up_out, mid_out,
    mats, srcs, seg, traces, fields, forces, my_trace, my_field, place, prof_v, prof_s,
    mat_sem, src_sem, z_sem, y_sem, b_sem, a_sem, sib_sem,
    w1_send, b_send, a_send, sib_send, tr_send, tr_recv, mid_send, mid_recv, p_send, p_recv, p_local,
):
    layers = 4
    r = lax.axis_index("range")
    d = lax.axis_index("depth")
    y, z, c = d // (Z * CORES), (d // CORES) % Z, d % CORES

    def at(yy, zz, cc):
        return (r, ((yy % Y) * Z + zz % Z) * CORES + cc)

    sibling = at(y, z, 1 - c)

    barrier = pltpu.get_barrier_semaphore()
    peers = [at(y, z + k, c) for k in range(1, Z)] + [at(y + k, z, c) for k in range(1, Y)] + [sibling]
    peers += [((r + k) % layers, d) for k in range(1, layers)]
    for peer in peers:
        pl.semaphore_signal(barrier, inc=1, device_id=peer, device_id_type=MESH)

    src_copies = [
        pltpu.make_async_copy(ref, srcs.at[i], src_sem.at[i]) for i, ref in enumerate((s_bottom, s_top))
    ]
    mat_copies = [
        pltpu.make_async_copy(ref, mats.at[i // 2, i % 2], mat_sem.at[i])
        for i, ref in enumerate((t_down, f_top, t_up, f_bottom))
    ]
    for copy in src_copies + mat_copies:
        copy.start()

    my_profile = profile[0]
    prof_v[r] = jnp.full(prof_v.shape[1:], my_profile, jnp.int32)

    every = depth[...]
    pick_s = lax.broadcasted_iota(jnp.int32, (256, 128), 0)
    pick_j = lax.broadcasted_iota(jnp.int32, (256, 128), 1)
    pick = jnp.where(pick_s == 4 * (pick_j % 64) + r, 1.0, 0.0).astype(BF16)
    high = jnp.broadcast_to(every // 64, (16, 256)).astype(F32).astype(BF16)
    low = jnp.broadcast_to(every % 64, (16, 256)).astype(F32).astype(BF16)
    chosen = jnp.dot(high, pick, preferred_element_type=F32) * 64.0 + jnp.dot(low, pick, preferred_element_type=F32)
    chosen = chosen[0:1].astype(jnp.int32)

    for copy in src_copies:
        copy.wait()
    lane = lax.broadcasted_iota(jnp.int32, (64, 128), 1)
    total = jnp.zeros((256, 128), F32)
    step = 1024
    for k0 in range(0, 4096, step):
        rows = lax.broadcasted_iota(jnp.int32, (step, 128), 0) + k0
        hot = jnp.where(rows == chosen, 1.0, 0.0).astype(BF16)
        left = srcs[:, my_profile, :, :, pl.ds(k0, step)].reshape(256, step)
        total += jnp.dot(left, hot, preferred_element_type=F32)
    total = total.reshape(2, 2, 64, 128)
    for i in range(2):
        forces[i] = jnp.where(lane < 64, total[i, 0], total[i, 1]).astype(BF16)

    middle = jnp.logical_or(r == 1, r == 2)
    way_01 = jnp.where(r < 2, 0, 1)
    way_2 = jnp.where(r % 2 == 0, 0, 1)
    ways = (way_01, way_01, way_2)
    layer_of = (jnp.where(r % 2 == 0, 1, 2), jnp.where(r < 2, r + 2, r - 2), jnp.where(r % 2 == 0, 3, 0))

    pl.semaphore_wait(barrier, len(peers))

    profile_copies = [
        pltpu.make_async_remote_copy(
            src_ref=prof_v.at[r], dst_ref=prof_v.at[r], send_sem=p_send.at[k], recv_sem=p_recv.at[r],
            device_id=((r + k) % layers, d), device_id_type=MESH,
        )
        for k in range(1, layers)
    ]

    def block(k, yy, zz, low=0, count=64):
        return seg.at[k, (yy % Y) * Z + zz % Z, c, pl.ds(low, count)]

    def row(k, yy, core):
        return seg.at[k, pl.ds((yy % Y) * Z, Z), core]

    def put(ref, send, recv, to):
        pltpu.make_async_remote_copy(
            src_ref=ref, dst_ref=ref, send_sem=send, recv_sem=recv, device_id=to, device_id_type=MESH
        ).start()

    def send_own(k):
        own = block(k, y, z)
        for i, dz in enumerate(DZ):
            put(own, w1_send.at[k], z_sem.at[k, i], at(y, z + dz, c))
        for j, dy in enumerate(DY):
            put(own, w1_send.at[k], y_sem.at[k, j], at(y + dy, z, c))

    def pass_y(k, j):
        got = DY[j]
        wait_bytes(block(k, y - got, z), y_sem.at[k, j])
        for dz in DZ:
            put(block(k, y - got, z, 0, PART), a_send.at[k], a_sem.at[k, j], at(y, z + dz, c))

    def pass_z(k, i):
        got = DZ[i]
        wait_bytes(block(k, y, z - got), z_sem.at[k, i])
        for j, dy in enumerate(DY):
            put(block(k, y, z - got, PART, 64 - PART), b_send.at[k], b_sem.at[k, j], at(y + dy, z, c))

    def multiply(k, kind, yy, prof):
        left = mats[ways[k], kind, prof, :, :, pl.ds(pl.multiple_of(yy * 1024, 1024), 1024)]
        right = seg[k, pl.ds(yy * Z, Z)].reshape(1024, 128)
        return jnp.dot(left.reshape(128, 1024), right, preferred_element_type=F32)

    def collect(k, prof):
        pass_y(k, 1)
        pass_y(k, 2)
        pass_z(k, 5)
        pass_z(k, 6)
        pass_y(k, 0)
        for i in (3, 4, 1, 2, 0):
            pass_z(k, i)
        put(row(k, y, c), sib_send.at[k], sib_sem.at[k, 3], sibling)
        for j in NEAR_Y:
            wait_bytes(seg.at[k, pl.ds(0, Z - 1), c, pl.ds(PART, 64 - PART)], b_sem.at[k, j])
            wait_bytes(seg.at[k, pl.ds(0, Z - 1), c, pl.ds(0, PART)], a_sem.at[k, j])
            put(row(k, y - DY[j], c), sib_send.at[k], sib_sem.at[k, j], sibling)
        total = jnp.zeros((128, 128), F32)
        for j in (3,) + NEAR_Y:
            yy = (y - (DY + (0,))[j]) % Y
            wait_bytes(row(k, yy, 1 - c), sib_sem.at[k, j])
            total += multiply(k, 0, yy, prof)
        return rotate_parts(total)

    def field(k, prof):
        total = jnp.zeros((128, 128), F32)
        for yy in range(Y):
            total += multiply(k, 1, yy, prof)
        return rotate_parts(total)

    def to_layer(k, mine, send, theirs, recv):
        return pltpu.make_async_remote_copy(
            src_ref=mine.at[k], dst_ref=theirs.at[r], send_sem=send.at[k], recv_sem=recv.at[r],
            device_id=(layer_of[k], d), device_id_type=MESH,
        )

    trace_copies = [to_layer(k, my_trace, tr_send, traces, tr_recv) for k in range(3)]
    field_copies = [to_layer(k, my_field, mid_send, fields, mid_recv) for k in range(3)]

    seg[0, y * Z + z, c] = forces[way_01]
    send_own(0)
    for copy in profile_copies:
        copy.start()

    i_in = lax.broadcasted_iota(jnp.int32, (512, 512), 0)
    i_out = lax.broadcasted_iota(jnp.int32, (512, 512), 1)
    goal = ((i_in % 128) // 64) * 256 + 4 * (i_in % 64) + i_in // 128
    place[...] = jnp.where(i_out == goal, 1.0, 0.0).astype(BF16)
    fields[r] = jnp.zeros((64, 128), F32)

    for copy in mat_copies:
        copy.wait()
    for k in range(1, layers):
        other = (r + k) % layers
        wait_bytes(prof_v.at[other], p_recv.at[other])
    to_scalar = pltpu.make_async_copy(prof_v, prof_s, p_local)
    for copy in profile_copies:
        copy.wait_send()
    to_scalar.start()
    to_scalar.wait()

    for k in range(3):
        prof = prof_s[layer_of[k], 0, 0]
        trace = collect(k, prof).astype(BF16)
        my_trace[k] = trace
        if k == 0:
            seg[1, y * Z + z, c] = trace
        elif k == 1:
            seg[2, y * Z + z, c] = jnp.where(middle, forces[1 - way_01], trace)
        if k < 2:
            send_own(k + 1)
        trace_copies[k].start()
        my_field[k] = field(k, prof)
        field_copies[k].start()

    for k in range(1, layers):
        other = (r + k) % layers
        wait_bytes(traces.at[other], tr_recv.at[other])
    traces[r] = forces[0]
    empty = jnp.zeros((64, 128), BF16)
    down = [jnp.where(i <= r, traces[i], empty) for i in range(layers)]
    traces[r] = forces[1]
    up = [jnp.where(i >= r, traces[i], empty) for i in range(layers)]
    both = jnp.concatenate([jnp.concatenate(down, axis=1), jnp.concatenate(up, axis=1)], axis=0)
    moved = jnp.dot(both, place[...], preferred_element_type=F32).astype(BF16)
    for part in range(2):
        down_out[0, part] = moved[:64, part * 256:(part + 1) * 256]
        up_out[0, part] = moved[64:, part * 256:(part + 1) * 256]

    for k in range(1, layers):
        other = (r + k) % layers
        wait_bytes(fields.at[other], mid_recv.at[other])
    whole = jnp.concatenate([fields[i] for i in range(layers)], axis=1)
    first = whole.astype(BF16)
    rest = whole - first.astype(F32)
    second = rest.astype(BF16)
    third = (rest - second.astype(F32)).astype(BF16)
    pieces = jnp.concatenate([first, second, third], axis=0)
    moved = jnp.dot(pieces, place[...], preferred_element_type=F32)
    moved = moved[0:64] + moved[64:128] + moved[128:192]
    for part in range(2):
        mid_out[0, part] = moved[:, part * 256:(part + 1) * 256]

    for k in range(3):
        wait_bytes(seg.at[k, pl.ds(0, 5)], w1_send.at[k])
        wait_bytes(seg.at[k, pl.ds(0, 21), 0, pl.ds(0, 64 - PART)], b_send.at[k])
        wait_bytes(seg.at[k, pl.ds(0, 21), 0, pl.ds(0, PART)], a_send.at[k])
        wait_bytes(seg.at[k, :, 0], sib_send.at[k])
        trace_copies[k].wait_send()
        field_copies[k].wait_send()


def body(
    transfer_down, transfer_up, field_from_top, field_from_bottom, source_to_bottom, source_to_top, profile, source_depth,
):
    hbm = pl.BlockSpec(memory_space=pl.ANY)
    vmem = pl.BlockSpec(memory_space=pltpu.VMEM)
    dma = pltpu.SemaphoreType.DMA
    return pl.pallas_call(
        kernel,
        out_shape=(
            jax.ShapeDtypeStruct((1, 2, 64, 256), BF16),
            jax.ShapeDtypeStruct((1, 2, 64, 256), BF16),
            jax.ShapeDtypeStruct((1, 2, 64, 256), F32),
        ),
        in_specs=[pl.BlockSpec(memory_space=pltpu.SMEM), vmem] + [hbm] * 6,
        out_specs=(vmem, vmem, vmem),
        scratch_shapes=[
            pltpu.VMEM((2, 2, 2, 2, 64, 4096), BF16),
            pltpu.VMEM((2, 2, 2, 64, 4096), BF16),
            pltpu.VMEM((3, Y * Z, CORES, 64, 128), BF16),
            pltpu.VMEM((4, 64, 128), BF16),
            pltpu.VMEM((4, 64, 128), F32),
            pltpu.VMEM((2, 64, 128), BF16),
            pltpu.VMEM((3, 64, 128), BF16),
            pltpu.VMEM((3, 64, 128), F32),
            pltpu.VMEM((512, 512), BF16),
            pltpu.VMEM((4, 8, 128), jnp.int32),
            pltpu.SMEM((4, 8, 128), jnp.int32),
            dma((4,)), dma((2,)),
            dma((3, 7)), dma((3, 3)), dma((3, 3)), dma((3, 3)), dma((3, 4)),
            dma((3,)), dma((3,)), dma((3,)), dma((3,)),
            dma((3,)), dma((4,)), dma((3,)), dma((4,)),
            dma((4,)), dma((4,)), dma(()),
        ],
        compiler_params=pltpu.CompilerParams(
            collective_id=0, has_side_effects=True, vmem_limit_bytes=60 * 2**20
        ),
        cost_estimate=pl.CostEstimate(flops=10**9, bytes_accessed=13 * 2**20, transcendentals=0),
        name="sweeps",
    )(
        profile, source_depth.reshape(1, 256),
        transfer_down, transfer_up, field_from_top, field_from_bottom, source_to_bottom, source_to_top,
    )


def solution(mesh):
    rows = P(None, None, "depth", None)
    return jax.shard_map(
        body,
        mesh=mesh,
        in_specs=(rows,) * 6 + (P("range"), P()),
        out_specs=(P("range", None, "depth", None),) * 3,
        check_vma=False,
    )
```

```python
import functools

import jax
import jax.numpy as jnp
from jax import lax
from jax.experimental import pallas as pl
from jax.experimental.pallas import tpu as pltpu
from jax.sharding import PartitionSpec as P

MESH = pl.DeviceIdType.MESH
Y, Z, CORES = 4, 8, 2
FAR_FIRST = [(dy, dz) for dy in (0, 1, -1, 2) for dz in (0, 1, -1, 2, -2, 3, -3, 4) if (dy, dz) != (0, 0)]
FAR_FIRST.sort(key=lambda o: -abs(o[0]) - abs(o[1]))
STRAIGHT = [o for o in FAR_FIRST if 0 in o]
OFFSETS = sorted(FAR_FIRST, key=lambda o: abs(o[0]) + abs(o[1]) + (0 if 0 in o else 3.6))
CHUNK, HALF = 1024, 2048
BF16, F32 = jnp.bfloat16, jnp.float32


def wait_bytes(ref, sem):
    pltpu.make_async_copy(ref, ref, sem).wait()


def rotate_parts(product):
    rows, columns = product.shape[0] // 2, product.shape[1]
    swapped = pltpu.roll(product[rows:], columns // 2, 1)
    lane = lax.broadcasted_iota(jnp.int32, swapped.shape, 1)
    return product[:rows] + jnp.where(lane < columns // 2, -swapped, swapped)


def kernel(
    profile, depth, t_down, t_up, f_top, f_bottom, s_bottom, s_top,
    down_out, up_out, mid_out,
    mats, src_0, src_1, src_2, src_3, seg, traces, fields, forces, my_trace, my_field, place, prof_v, prof_s,
    hot, mat_sem, src_sem, seg_send, seg_recv, sib_recv, tr_send, tr_recv, mid_send, mid_recv, p_send, p_recv, p_local,
):
    layers = 4
    srcs = (src_0, src_1, src_2, src_3)
    r = lax.axis_index("range")
    d = lax.axis_index("depth")
    y, z, c = d // (Z * CORES), (d // CORES) % Z, d % CORES

    def at(yy, zz, cc):
        return (r, ((yy % Y) * Z + zz % Z) * CORES + cc)

    sibling = at(y, z, 1 - c)

    barrier = pltpu.get_barrier_semaphore()
    peers = [at(y, z + k, c) for k in range(1, Z)] + [at(y + k, z, c) for k in range(1, Y)] + [sibling]
    peers += [((r + k) % layers, d) for k in range(1, layers)]
    for peer in peers:
        pl.semaphore_signal(barrier, inc=1, device_id=peer, device_id_type=MESH)

    down_first = r < 2
    way_01 = jnp.where(down_first, 0, 1)

    src_copies = [
        [
            pltpu.make_async_copy(ref.at[:, :, :, pl.ds(half * HALF, HALF)], srcs[2 * i + half], src_sem.at[i, half])
            for i, ref in enumerate(refs) for half in range(2)
        ]
        for refs in ((s_bottom, s_top), (s_top, s_bottom))
    ]
    for way in range(2):
        @pl.when(way_01 == way)
        def _():
            for copy in src_copies[way]:
                copy.start()
    mat_copies = [
        pltpu.make_async_copy(ref, mats.at[i // 2, i % 2], mat_sem.at[i])
        for i, ref in enumerate((t_down, f_top, t_up, f_bottom))
    ]

    my_profile = profile[0]
    prof_v[r] = jnp.full(prof_v.shape[1:], my_profile, jnp.int32)

    every = depth[...]
    pick_s = lax.broadcasted_iota(jnp.int32, (256, 128), 0)
    pick_j = lax.broadcasted_iota(jnp.int32, (256, 128), 1)
    pick = jnp.where(pick_s == 4 * (pick_j % 64) + r, 1.0, 0.0).astype(BF16)
    high = jnp.broadcast_to(every // 64, (16, 256)).astype(F32).astype(BF16)
    low = jnp.broadcast_to(every % 64, (16, 256)).astype(F32).astype(BF16)
    chosen = jnp.dot(high, pick, preferred_element_type=F32) * 64.0 + jnp.dot(low, pick, preferred_element_type=F32)
    chosen = chosen[0:1].astype(jnp.int32)

    for k0 in range(0, 4096, CHUNK):
        rows = lax.broadcasted_iota(jnp.int32, (CHUNK, 128), 0) + k0
        hot[pl.ds(k0, CHUNK)] = jnp.where(rows == chosen, 1.0, 0.0).astype(BF16)
    lane = lax.broadcasted_iota(jnp.int32, (64, 128), 1)

    def find_force(i):
        total = jnp.zeros((128, 128), F32)
        for half in range(2):
            src = srcs[2 * i + half]
            wait_bytes(src, src_sem.at[i, half])
            total += jnp.dot(
                src[my_profile].reshape(128, HALF), hot[pl.ds(half * HALF, HALF)], preferred_element_type=F32
            )
        return jnp.where(lane < 64, total[:64], total[64:]).astype(BF16)

    middle = jnp.logical_or(r == 1, r == 2)
    way_2 = jnp.where(r % 2 == 0, 0, 1)
    ways = (way_01, way_01, way_2)
    layer_of = (jnp.where(r % 2 == 0, 1, 2), jnp.where(r < 2, r + 2, r - 2), jnp.where(r % 2 == 0, 3, 0))

    profile_copies = [
        pltpu.make_async_remote_copy(
            src_ref=prof_v.at[r], dst_ref=prof_v.at[r], send_sem=p_send.at[k], recv_sem=p_recv.at[r],
            device_id=((r + k) % layers, d), device_id_type=MESH,
        )
        for k in range(1, layers)
    ]

    def block(k, offset):
        return seg.at[k, ((y - offset[0]) % Y) * Z + (z - offset[1]) % Z, c]

    def row(k, yy, core):
        return seg.at[k, pl.ds((yy % Y) * Z, Z), core]

    def put(ref, send, recv, to):
        pltpu.make_async_remote_copy(
            src_ref=ref, dst_ref=ref, send_sem=send, recv_sem=recv, device_id=to, device_id_type=MESH
        ).start()

    def ship(k, held, offset):
        put(
            block(k, held), seg_send.at[k], seg_recv.at[k, (offset[0] % Y) * Z + offset[1] % Z],
            at(y + offset[0] - held[0], z + offset[1] - held[1], c),
        )

    def to_sibling(k, held):
        put(block(k, held), seg_send.at[k], sib_recv.at[k, held[0] % Y], sibling)

    def send_own(k):
        for offset in STRAIGHT:
            ship(k, (0, 0), offset)
        to_sibling(k, (0, 0))

    def pass_on(k, held):
        wait_bytes(block(k, held), seg_recv.at[k, (held[0] % Y) * Z + held[1] % Z])
        for offset in FAR_FIRST:
            if 0 not in offset:
                if (offset[0], 0) == held if abs(offset[1]) <= 2 else (0, offset[1]) == held:
                    ship(k, held, offset)
        to_sibling(k, held)

    def multiply(k, kind, yy, prof):
        left = mats[ways[k], kind, prof, :, :, pl.ds(pl.multiple_of(yy * 1024, 1024), 1024)]
        right = seg[k, pl.ds(yy * Z, Z)].reshape(1024, 128)
        return jnp.dot(left.reshape(128, 1024), right, preferred_element_type=F32)

    def collect(k, prof):
        for held in OFFSETS:
            pass_on(k, held)
        total = jnp.zeros((128, 128), F32)
        for dy in (0, 1, -1, 2):
            yy = (y - dy) % Y
            wait_bytes(row(k, yy, 1 - c), sib_recv.at[k, dy % Y])
            total += multiply(k, 0, yy, prof)
        return rotate_parts(total)

    def field(k, prof):
        total = jnp.zeros((128, 128), F32)
        for yy in range(Y):
            total += multiply(k, 1, yy, prof)
        return rotate_parts(total)

    def to_layer(k, mine, send, theirs, recv):
        return pltpu.make_async_remote_copy(
            src_ref=mine.at[k], dst_ref=theirs.at[r], send_sem=send.at[k], recv_sem=recv.at[r],
            device_id=(layer_of[k], d), device_id_type=MESH,
        )

    trace_copies = [to_layer(k, my_trace, tr_send, traces, tr_recv) for k in range(3)]
    field_copies = [to_layer(k, my_field, mid_send, fields, mid_recv) for k in range(3)]

    force = find_force(0)
    seg[0, y * Z + z, c] = force
    pl.semaphore_wait(barrier, len(peers))
    send_own(0)
    for copy in mat_copies:
        copy.start()
    forces[way_01] = force
    forces[1 - way_01] = find_force(1)
    for copy in profile_copies:
        copy.start()

    i_in = lax.broadcasted_iota(jnp.int32, (512, 512), 0)
    i_out = lax.broadcasted_iota(jnp.int32, (512, 512), 1)
    goal = ((i_in % 128) // 64) * 256 + 4 * (i_in % 64) + i_in // 128
    place[...] = jnp.where(i_out == goal, 1.0, 0.0).astype(BF16)
    fields[r] = jnp.zeros((64, 128), F32)

    for copy in mat_copies:
        copy.wait()
    for k in range(1, layers):
        other = (r + k) % layers
        wait_bytes(prof_v.at[other], p_recv.at[other])
    to_scalar = pltpu.make_async_copy(prof_v, prof_s, p_local)
    for copy in profile_copies:
        copy.wait_send()
    to_scalar.start()
    to_scalar.wait()

    for k in range(3):
        prof = prof_s[layer_of[k], 0, 0]
        trace = collect(k, prof).astype(BF16)
        my_trace[k] = trace
        if k == 0:
            seg[1, y * Z + z, c] = trace
        elif k == 1:
            seg[2, y * Z + z, c] = jnp.where(middle, forces[1 - way_01], trace)
        if k < 2:
            send_own(k + 1)
        trace_copies[k].start()
        my_field[k] = field(k, prof)
        field_copies[k].start()

    for k in range(1, layers):
        other = (r + k) % layers
        wait_bytes(traces.at[other], tr_recv.at[other])
    traces[r] = forces[0]
    empty = jnp.zeros((64, 128), BF16)
    down = [jnp.where(i <= r, traces[i], empty) for i in range(layers)]
    traces[r] = forces[1]
    up = [jnp.where(i >= r, traces[i], empty) for i in range(layers)]
    both = jnp.concatenate([jnp.concatenate(down, axis=1), jnp.concatenate(up, axis=1)], axis=0)
    moved = jnp.dot(both, place[...], preferred_element_type=F32).astype(BF16)
    for part in range(2):
        down_out[0, part] = moved[:64, part * 256:(part + 1) * 256]
        up_out[0, part] = moved[64:, part * 256:(part + 1) * 256]

    for k in range(1, layers):
        other = (r + k) % layers
        wait_bytes(fields.at[other], mid_recv.at[other])
    whole = jnp.concatenate([fields[i] for i in range(layers)], axis=1)
    first = whole.astype(BF16)
    rest = whole - first.astype(F32)
    second = rest.astype(BF16)
    third = (rest - second.astype(F32)).astype(BF16)
    pieces = jnp.concatenate([first, second, third], axis=0)
    moved = jnp.dot(pieces, place[...], preferred_element_type=F32)
    moved = moved[0:64] + moved[64:128] + moved[128:192]
    for part in range(2):
        mid_out[0, part] = moved[:, part * 256:(part + 1) * 256]

    for k in range(3):
        wait_bytes(seg.at[:, pl.ds(0, 21), 0], seg_send.at[k])
        trace_copies[k].wait_send()
        field_copies[k].wait_send()


def store(down, up, mid, down_out, up_out, mid_out, sem):
    copies = [
        pltpu.make_async_copy(src, dst, sem.at[i])
        for i, (src, dst) in enumerate(((mid, mid_out), (down, down_out), (up, up_out)))
    ]
    for copy in copies:
        copy.start()
    for copy in copies:
        copy.wait()


def body(
    transfer_down, transfer_up, field_from_top, field_from_bottom, source_to_bottom, source_to_top, profile, source_depth,
):
    hbm = pl.BlockSpec(memory_space=pl.ANY)
    vmem = pl.BlockSpec(memory_space=pltpu.VMEM)
    dma = pltpu.SemaphoreType.DMA
    outs = (
        jax.ShapeDtypeStruct((1, 2, 64, 256), BF16),
        jax.ShapeDtypeStruct((1, 2, 64, 256), BF16),
        jax.ShapeDtypeStruct((1, 2, 64, 256), F32),
    )
    results = pl.pallas_call(
        kernel,
        out_shape=outs,
        in_specs=[pl.BlockSpec(memory_space=pltpu.SMEM), vmem] + [hbm] * 6,
        out_specs=(vmem, vmem, vmem),
        scratch_shapes=[
            pltpu.VMEM((2, 2, 2, 2, 64, 4096), BF16),
            *[pltpu.VMEM((2, 2, 64, HALF), BF16)] * 4,
            pltpu.VMEM((3, Y * Z, CORES, 64, 128), BF16),
            pltpu.VMEM((4, 64, 128), BF16),
            pltpu.VMEM((4, 64, 128), F32),
            pltpu.VMEM((2, 64, 128), BF16),
            pltpu.VMEM((3, 64, 128), BF16),
            pltpu.VMEM((3, 64, 128), F32),
            pltpu.VMEM((512, 512), BF16),
            pltpu.VMEM((4, 8, 128), jnp.int32),
            pltpu.SMEM((4, 8, 128), jnp.int32),
            pltpu.VMEM((4096, 128), BF16),
            dma((4,)), dma((2, 2)),
            dma((3,)), dma((3, Y * Z)), dma((3, Y)),
            dma((3,)), dma((4,)), dma((3,)), dma((4,)),
            dma((4,)), dma((4,)), dma(()),
        ],
        compiler_params=pltpu.CompilerParams(
            collective_id=0, has_side_effects=True, vmem_limit_bytes=60 * 2**20
        ),
        cost_estimate=pl.CostEstimate(flops=10**9, bytes_accessed=13 * 2**20, transcendentals=0),
        name="sweeps",
    )(
        profile, source_depth.reshape(1, 256),
        transfer_down, transfer_up, field_from_top, field_from_bottom, source_to_bottom, source_to_top,
    )
    return pl.pallas_call(
        store,
        out_shape=outs,
        in_specs=[vmem] * 3,
        out_specs=(hbm,) * 3,
        scratch_shapes=[dma((3,))],
        name="store",
    )(*results)


def solution(mesh):
    rows = P(None, None, "depth", None)
    return jax.shard_map(
        body,
        mesh=mesh,
        in_specs=(rows,) * 6 + (P("range"), P()),
        out_specs=(P("range", None, "depth", None),) * 3,
        check_vma=False,
    )
```

```python
import functools

import jax
import jax.numpy as jnp
from jax import lax
from jax.experimental import pallas as pl
from jax.experimental.pallas import tpu as pltpu
from jax.sharding import PartitionSpec as P

MESH = pl.DeviceIdType.MESH
Y, Z, CORES = 4, 8, 2
FAR_FIRST = [(dy, dz) for dy in (0, 1, -1, 2) for dz in (0, 1, -1, 2, -2, 3, -3, 4) if (dy, dz) != (0, 0)]
FAR_FIRST.sort(key=lambda o: -abs(o[0]) - abs(o[1]))
STRAIGHT = [o for o in FAR_FIRST if 0 in o]
OFFSETS = sorted(FAR_FIRST, key=lambda o: abs(o[0]) + abs(o[1]) + (0 if 0 in o else 3.6))
ORDER = [(0, 0)] + OFFSETS
GROUPS = {26: (0, 20), 31: (20, 32)}
CHUNK, HALF = 1024, 2048
BF16, F32 = jnp.bfloat16, jnp.float32


def wait_bytes(ref, sem):
    pltpu.make_async_copy(ref, ref, sem).wait()


def rotate_parts(product):
    rows, columns = product.shape[0] // 2, product.shape[1]
    swapped = pltpu.roll(product[rows:], columns // 2, 1)
    lane = lax.broadcasted_iota(jnp.int32, swapped.shape, 1)
    return product[:rows] + jnp.where(lane < columns // 2, -swapped, swapped)


def kernel(
    profile, depth, t_down, t_up, f_top, f_bottom, s_bottom, s_top,
    down_out, up_out, mid_out,
    mats, src_0, src_1, src_2, src_3, seg, traces, fields, forces, my_trace, my_field, place, prof_v, prof_s,
    hot, own_profile, depth_v, small_sem, mat_sem, src_sem, seg_send, seg_recv, sib_recv, tr_send, tr_recv, mid_send, mid_recv, p_send, p_recv, p_local,
):
    layers = 4
    srcs = (src_0, src_1, src_2, src_3)
    r = lax.axis_index("range")
    d = lax.axis_index("depth")
    y, z, c = d // (Z * CORES), (d // CORES) % Z, d % CORES

    def at(yy, zz, cc):
        return (r, ((yy % Y) * Z + zz % Z) * CORES + cc)

    sibling = at(y, z, 1 - c)

    barrier = pltpu.get_barrier_semaphore()
    peers = [at(y, z + k, c) for k in range(1, Z)] + [at(y + k, z, c) for k in range(1, Y)] + [sibling]
    peers += [((r + k) % layers, d) for k in range(1, layers)]
    for peer in peers:
        pl.semaphore_signal(barrier, inc=1, device_id=peer, device_id_type=MESH)

    down_first = r < 2
    way_01 = jnp.where(down_first, 0, 1)

    src_copies = [
        [
            pltpu.make_async_copy(ref.at[:, :, :, pl.ds(half * HALF, HALF)], srcs[2 * i + half], src_sem.at[i, half])
            for i, ref in enumerate(refs) for half in range(2)
        ]
        for refs in ((s_bottom, s_top), (s_top, s_bottom))
    ]
    for way in range(2):
        @pl.when(way_01 == way)
        def _():
            for copy in src_copies[way]:
                copy.start()
    mat_copies = [
        pltpu.make_async_copy(
            ref.at[:, :, :, pl.ds(pl.multiple_of((((y - dy) % Y) * Z + (z - dz) % Z) * 128, 128), 128)],
            mats.at[i // 2, i % 2, :, :, :, pl.ds(place_in * 128, 128)],
            mat_sem.at[i],
        )
        for i, ref in enumerate((t_down, f_top, t_up, f_bottom)) for place_in, (dy, dz) in enumerate(ORDER)
    ]

    copies = [pltpu.make_async_copy(profile, own_profile, small_sem.at[0]), pltpu.make_async_copy(depth, depth_v, small_sem.at[1])]
    for copy in copies:
        copy.start()
    for copy in copies:
        copy.wait()
    my_profile = own_profile[0]
    prof_v[r] = jnp.full(prof_v.shape[1:], my_profile, jnp.int32)

    every = depth_v[...]
    pick_s = lax.broadcasted_iota(jnp.int32, (256, 128), 0)
    pick_j = lax.broadcasted_iota(jnp.int32, (256, 128), 1)
    pick = jnp.where(pick_s == 4 * (pick_j % 64) + r, 1.0, 0.0).astype(BF16)
    high = jnp.broadcast_to(every // 64, (16, 256)).astype(F32).astype(BF16)
    low = jnp.broadcast_to(every % 64, (16, 256)).astype(F32).astype(BF16)
    chosen = jnp.dot(high, pick, preferred_element_type=F32) * 64.0 + jnp.dot(low, pick, preferred_element_type=F32)
    chosen = chosen[0:1].astype(jnp.int32)

    for k0 in range(0, 4096, CHUNK):
        rows = lax.broadcasted_iota(jnp.int32, (CHUNK, 128), 0) + k0
        hot[pl.ds(k0, CHUNK)] = jnp.where(rows == chosen, 1.0, 0.0).astype(BF16)
    lane = lax.broadcasted_iota(jnp.int32, (64, 128), 1)

    def find_force(i):
        total = jnp.zeros((128, 128), F32)
        for half in range(2):
            src = srcs[2 * i + half]
            wait_bytes(src, src_sem.at[i, half])
            total += jnp.dot(
                src[my_profile].reshape(128, HALF), hot[pl.ds(half * HALF, HALF)], preferred_element_type=F32
            )
        return jnp.where(lane < 64, total[:64], total[64:]).astype(BF16)

    middle = jnp.logical_or(r == 1, r == 2)
    way_2 = jnp.where(r % 2 == 0, 0, 1)
    ways = (way_01, way_01, way_2)
    layer_of = (jnp.where(r % 2 == 0, 1, 2), jnp.where(r < 2, r + 2, r - 2), jnp.where(r % 2 == 0, 3, 0))

    profile_copies = [
        pltpu.make_async_remote_copy(
            src_ref=prof_v.at[r], dst_ref=prof_v.at[r], send_sem=p_send.at[k], recv_sem=p_recv.at[r],
            device_id=((r + k) % layers, d), device_id_type=MESH,
        )
        for k in range(1, layers)
    ]

    def block(k, offset):
        return seg.at[k, ((y - offset[0]) % Y) * Z + (z - offset[1]) % Z, c]

    def sib_block(k, offset):
        return seg.at[k, ((y - offset[0]) % Y) * Z + (z - offset[1]) % Z, 1 - c]

    def index(offset):
        return (offset[0] % Y) * Z + offset[1] % Z

    def put(ref, send, recv, to):
        pltpu.make_async_remote_copy(
            src_ref=ref, dst_ref=ref, send_sem=send, recv_sem=recv, device_id=to, device_id_type=MESH
        ).start()

    def ship(k, held, offset):
        put(
            block(k, held), seg_send.at[k], seg_recv.at[k, index(offset)],
            at(y + offset[0] - held[0], z + offset[1] - held[1], c),
        )

    def to_sibling(k, held):
        put(block(k, held), seg_send.at[k], sib_recv.at[k, index(held)], sibling)

    def send_own(k):
        for offset in STRAIGHT:
            ship(k, (0, 0), offset)
        to_sibling(k, (0, 0))

    def pass_on(k, held):
        wait_bytes(block(k, held), seg_recv.at[k, index(held)])
        for offset in FAR_FIRST:
            if 0 not in offset:
                if (offset[0], 0) == held if abs(offset[1]) <= 2 else (0, offset[1]) == held:
                    ship(k, held, offset)
        to_sibling(k, held)

    def get_ready():
        for i in range(4):
            wait_bytes(mats.at[i // 2, i % 2], mat_sem.at[i])
        for k in range(1, layers):
            other = (r + k) % layers
            wait_bytes(prof_v.at[other], p_recv.at[other])
        for copy in profile_copies:
            copy.wait_send()
        to_scalar = pltpu.make_async_copy(prof_v, prof_s, p_local)
        to_scalar.start()
        to_scalar.wait()

    def multiply(k, kind, group, prof):
        first, end = group
        left = mats[ways[k], kind, prof, :, :, pl.ds(first * 128, (end - first) * 128)]
        right = [seg[k, ((y - dy) % Y) * Z + (z - dz) % Z].reshape(128, 128) for dy, dz in ORDER[first:end]]
        return jnp.dot(left.reshape(128, -1), jnp.concatenate(right, axis=0), preferred_element_type=F32)

    def collect(k):
        kinds = (0, 1) if k == 2 else (0,)
        totals = [jnp.zeros((128, 128), F32) for _ in kinds]
        for n, held in enumerate(OFFSETS, 1):
            pass_on(k, held)
            if n == len(STRAIGHT) and k == 0:
                get_ready()
            if n in GROUPS:
                for offset in ORDER[slice(*GROUPS[n])]:
                    wait_bytes(sib_block(k, offset), sib_recv.at[k, index(offset)])
                prof = prof_s[layer_of[k], 0, 0]
                for t, kind in enumerate(kinds):
                    totals[t] += multiply(k, kind, GROUPS[n], prof)
        return [rotate_parts(total) for total in totals]

    def field(k):
        prof = prof_s[layer_of[k], 0, 0]
        return rotate_parts(sum(multiply(k, 1, group, prof) for group in GROUPS.values()))

    def to_layer(k, mine, send, theirs, recv):
        return pltpu.make_async_remote_copy(
            src_ref=mine.at[k], dst_ref=theirs.at[r], send_sem=send.at[k], recv_sem=recv.at[r],
            device_id=(layer_of[k], d), device_id_type=MESH,
        )

    trace_copies = [to_layer(k, my_trace, tr_send, traces, tr_recv) for k in range(3)]
    field_copies = [to_layer(k, my_field, mid_send, fields, mid_recv) for k in range(3)]

    force = find_force(0)
    seg[0, y * Z + z, c] = force
    pl.semaphore_wait(barrier, len(peers))
    send_own(0)
    for copy in mat_copies:
        copy.start()
    forces[way_01] = force
    forces[1 - way_01] = find_force(1)
    for copy in profile_copies:
        copy.start()

    i_in = lax.broadcasted_iota(jnp.int32, (512, 512), 0)
    i_out = lax.broadcasted_iota(jnp.int32, (512, 512), 1)
    goal = ((i_in % 128) // 64) * 256 + 4 * (i_in % 64) + i_in // 128
    place[...] = jnp.where(i_out == goal, 1.0, 0.0).astype(BF16)
    fields[r] = jnp.zeros((64, 128), F32)

    for k in range(3):
        results = collect(k)
        trace = results[0].astype(BF16)
        my_trace[k] = trace
        if k == 0:
            seg[1, y * Z + z, c] = trace
        elif k == 1:
            seg[2, y * Z + z, c] = jnp.where(middle, forces[1 - way_01], trace)
        if k < 2:
            send_own(k + 1)
        trace_copies[k].start()
        my_field[k] = results[1] if k == 2 else field(k)
        field_copies[k].start()

    for k in range(1, layers):
        other = (r + k) % layers
        wait_bytes(traces.at[other], tr_recv.at[other])
    traces[r] = forces[0]
    empty = jnp.zeros((64, 128), BF16)
    down = [jnp.where(i <= r, traces[i], empty) for i in range(layers)]
    traces[r] = forces[1]
    up = [jnp.where(i >= r, traces[i], empty) for i in range(layers)]
    both = jnp.concatenate([jnp.concatenate(down, axis=1), jnp.concatenate(up, axis=1)], axis=0)
    moved = jnp.dot(both, place[...], preferred_element_type=F32).astype(BF16)
    for part in range(2):
        down_out[0, part] = moved[:64, part * 256:(part + 1) * 256]
        up_out[0, part] = moved[64:, part * 256:(part + 1) * 256]

    for k in range(1, layers):
        other = (r + k) % layers
        wait_bytes(fields.at[other], mid_recv.at[other])
    whole = jnp.concatenate([fields[i] for i in range(layers)], axis=1)
    first = whole.astype(BF16)
    rest = whole - first.astype(F32)
    second = rest.astype(BF16)
    third = (rest - second.astype(F32)).astype(BF16)
    pieces = jnp.concatenate([first, second, third], axis=0)
    moved = jnp.dot(pieces, place[...], preferred_element_type=F32)
    moved = moved[0:64] + moved[64:128] + moved[128:192]
    for part in range(2):
        mid_out[0, part] = moved[:, part * 256:(part + 1) * 256]

    for k in range(3):
        wait_bytes(seg.at[:, pl.ds(0, 21), 0], seg_send.at[k])
        trace_copies[k].wait_send()
        field_copies[k].wait_send()


def store(down, up, mid, down_out, up_out, mid_out, sem):
    copies = [
        pltpu.make_async_copy(src, dst, sem.at[i])
        for i, (src, dst) in enumerate(((mid, mid_out), (down, down_out), (up, up_out)))
    ]
    for copy in copies:
        copy.start()
    for copy in copies:
        copy.wait()


def body(
    transfer_down, transfer_up, field_from_top, field_from_bottom, source_to_bottom, source_to_top, profile, source_depth,
):
    hbm = pl.BlockSpec(memory_space=pl.ANY)
    vmem = pl.BlockSpec(memory_space=pltpu.VMEM)
    dma = pltpu.SemaphoreType.DMA
    outs = (
        jax.ShapeDtypeStruct((1, 2, 64, 256), BF16),
        jax.ShapeDtypeStruct((1, 2, 64, 256), BF16),
        jax.ShapeDtypeStruct((1, 2, 64, 256), F32),
    )
    results = pl.pallas_call(
        kernel,
        out_shape=tuple(pltpu.VMEM(o.shape, o.dtype) for o in outs),
        in_specs=[hbm] * 8,
        out_specs=(vmem, vmem, vmem),
        scratch_shapes=[
            pltpu.VMEM((2, 2, 2, 2, 64, 4096), BF16),
            *[pltpu.VMEM((2, 2, 64, HALF), BF16)] * 4,
            pltpu.VMEM((3, Y * Z, CORES, 64, 128), BF16),
            pltpu.VMEM((4, 64, 128), BF16),
            pltpu.VMEM((4, 64, 128), F32),
            pltpu.VMEM((2, 64, 128), BF16),
            pltpu.VMEM((3, 64, 128), BF16),
            pltpu.VMEM((3, 64, 128), F32),
            pltpu.VMEM((512, 512), BF16),
            pltpu.VMEM((4, 8, 128), jnp.int32),
            pltpu.SMEM((4, 8, 128), jnp.int32),
            pltpu.VMEM((4096, 128), BF16),
            pltpu.SMEM((1,), jnp.int32), pltpu.VMEM((1, 256), jnp.int32), dma((2,)),
            dma((4,)), dma((2, 2)),
            dma((3,)), dma((3, Y * Z)), dma((3, Y * Z)),
            dma((3,)), dma((4,)), dma((3,)), dma((4,)),
            dma((4,)), dma((4,)), dma(()),
        ],
        compiler_params=pltpu.CompilerParams(
            collective_id=0, has_side_effects=True, vmem_limit_bytes=60 * 2**20
        ),
        cost_estimate=pl.CostEstimate(flops=10**9, bytes_accessed=13 * 2**20, transcendentals=0),
        name="sweeps",
    )(
        profile, source_depth.reshape(1, 256),
        transfer_down, transfer_up, field_from_top, field_from_bottom, source_to_bottom, source_to_top,
    )
    return pl.pallas_call(
        store,
        out_shape=outs,
        in_specs=[vmem] * 3,
        out_specs=(hbm,) * 3,
        scratch_shapes=[dma((3,))],
        name="store",
    )(*[pltpu.with_memory_space_constraint(x, pltpu.VMEM) for x in results])


def solution(mesh):
    rows = P(None, None, "depth", None)
    return jax.shard_map(
        body,
        mesh=mesh,
        in_specs=(rows,) * 6 + (P("range"), P()),
        out_specs=(P("range", None, "depth", None),) * 3,
        check_vma=False,
    )
```

```python
import functools

import jax
import jax.numpy as jnp
from jax import lax
from jax.experimental import pallas as pl
from jax.experimental.pallas import tpu as pltpu
from jax.sharding import PartitionSpec as P

MESH = pl.DeviceIdType.MESH
Y, Z, CORES = 4, 8, 2
FAR_FIRST = [(dy, dz) for dy in (0, 1, -1, 2) for dz in (0, 1, -1, 2, -2, 3, -3, 4) if (dy, dz) != (0, 0)]
FAR_FIRST.sort(key=lambda o: -abs(o[0]) - abs(o[1]))
STRAIGHT = [o for o in FAR_FIRST if 0 in o]
OFFSETS = sorted(
    FAR_FIRST,
    key=lambda o: (0 not in o or 0 < abs(o[1]) <= 2, 0 not in o, o[1] != 0 and 0 in o, abs(o[0]) + abs(o[1])),
)
ORDER = [(0, 0)] + OFFSETS
GROUPS = {26: (0, 20), 31: (20, 32)}
CHUNK, HALF = 1024, 2048
BF16, F32 = jnp.bfloat16, jnp.float32


def wait_bytes(ref, sem):
    pltpu.make_async_copy(ref, ref, sem).wait()


def rotate_parts(product):
    rows, columns = product.shape[0] // 2, product.shape[1]
    swapped = pltpu.roll(product[rows:], columns // 2, 1)
    lane = lax.broadcasted_iota(jnp.int32, swapped.shape, 1)
    return product[:rows] + jnp.where(lane < columns // 2, -swapped, swapped)


def kernel(
    profile, depth, t_down, t_up, f_top, f_bottom, s_bottom, s_top,
    down_out, up_out, mid_out,
    mats, src_0, src_1, src_2, src_3, seg, traces, fields, forces, my_trace, my_field, place, prof_v, prof_s,
    hot, own_profile, depth_v, small_sem, mat_sem, src_sem, seg_send, seg_recv, sib_recv, tr_send, tr_recv, mid_send, mid_recv, p_send, p_recv, p_local, x_send,
):
    layers = 4
    srcs = (src_0, src_1, src_2, src_3)
    r = lax.axis_index("range")
    d = lax.axis_index("depth")
    y, z, c = d // (Z * CORES), (d // CORES) % Z, d % CORES

    def at(yy, zz, cc):
        return (r, ((yy % Y) * Z + zz % Z) * CORES + cc)

    sibling = at(y, z, 1 - c)

    barrier = pltpu.get_barrier_semaphore()
    peers = [at(y, z + k, c) for k in range(1, Z)] + [at(y + k, z, c) for k in range(1, Y)] + [sibling]
    peers += [((r + k) % layers, d) for k in range(1, layers)]
    for peer in peers:
        pl.semaphore_signal(barrier, inc=1, device_id=peer, device_id_type=MESH)

    down_first = r < 2
    way_01 = jnp.where(down_first, 0, 1)

    src_copies = [
        [
            pltpu.make_async_copy(ref.at[:, :, :, pl.ds(half * HALF, HALF)], srcs[2 * i + half], src_sem.at[i, half])
            for i, ref in enumerate(refs) for half in range(2)
        ]
        for refs in ((s_bottom, s_top), (s_top, s_bottom))
    ]
    for way in range(2):
        @pl.when(way_01 == way)
        def _():
            for copy in src_copies[way]:
                copy.start()
    mat_copies = [
        pltpu.make_async_copy(
            ref.at[:, :, :, pl.ds(pl.multiple_of((((y - dy) % Y) * Z + (z - dz) % Z) * 128, 128), 128)],
            mats.at[i // 2, i % 2, :, :, :, pl.ds(place_in * 128, 128)],
            mat_sem.at[i],
        )
        for i, ref in enumerate((t_down, f_top, t_up, f_bottom)) for place_in, (dy, dz) in enumerate(ORDER)
    ]

    copies = [pltpu.make_async_copy(profile, own_profile, small_sem.at[0]), pltpu.make_async_copy(depth, depth_v, small_sem.at[1])]
    for copy in copies:
        copy.start()
    for copy in copies:
        copy.wait()
    my_profile = own_profile[0]
    prof_v[r] = jnp.full(prof_v.shape[1:], my_profile, jnp.int32)

    every = depth_v[...]
    pick_s = lax.broadcasted_iota(jnp.int32, (256, 128), 0)
    pick_j = lax.broadcasted_iota(jnp.int32, (256, 128), 1)
    pick = jnp.where(pick_s == 4 * (pick_j % 64) + r, 1.0, 0.0).astype(BF16)
    high = jnp.broadcast_to(every // 64, (16, 256)).astype(F32).astype(BF16)
    low = jnp.broadcast_to(every % 64, (16, 256)).astype(F32).astype(BF16)
    chosen = jnp.dot(high, pick, preferred_element_type=F32) * 64.0 + jnp.dot(low, pick, preferred_element_type=F32)
    chosen = chosen[0:1].astype(jnp.int32)

    for k0 in range(0, 4096, CHUNK):
        rows = lax.broadcasted_iota(jnp.int32, (CHUNK, 128), 0) + k0
        hot[pl.ds(k0, CHUNK)] = jnp.where(rows == chosen, 1.0, 0.0).astype(BF16)
    lane = lax.broadcasted_iota(jnp.int32, (64, 128), 1)

    def find_force(i):
        total = jnp.zeros((128, 128), F32)
        for half in range(2):
            src = srcs[2 * i + half]
            wait_bytes(src, src_sem.at[i, half])
            total += jnp.dot(
                src[my_profile].reshape(128, HALF), hot[pl.ds(half * HALF, HALF)], preferred_element_type=F32
            )
        return jnp.where(lane < 64, total[:64], total[64:]).astype(BF16)

    middle = jnp.logical_or(r == 1, r == 2)
    outer = jnp.logical_not(middle)
    ways = (way_01, r % 2, 1 - r % 2)
    layer_of = (1 + r % 2, jnp.where(r == 0, 2, jnp.where(r == 1, 0, jnp.where(r == 2, 3, 1))), 3 * (r % 2))

    profile_copies = [
        pltpu.make_async_remote_copy(
            src_ref=prof_v.at[r], dst_ref=prof_v.at[r], send_sem=p_send.at[k], recv_sem=p_recv.at[r],
            device_id=((r + k) % layers, d), device_id_type=MESH,
        )
        for k in range(1, layers)
    ]

    def block(k, offset):
        return seg.at[k, ((y - offset[0]) % Y) * Z + (z - offset[1]) % Z, c]

    def sib_block(k, offset):
        return seg.at[k, ((y - offset[0]) % Y) * Z + (z - offset[1]) % Z, 1 - c]

    def index(offset):
        return (offset[0] % Y) * Z + offset[1] % Z

    def put(ref, send, recv, to):
        pltpu.make_async_remote_copy(
            src_ref=ref, dst_ref=ref, send_sem=send, recv_sem=recv, device_id=to, device_id_type=MESH
        ).start()

    def ship(k, held, offset):
        put(
            block(k, held), seg_send.at[k], seg_recv.at[k, index(offset)],
            at(y + offset[0] - held[0], z + offset[1] - held[1], c),
        )

    def to_sibling(k, held):
        put(block(k, held), seg_send.at[k], sib_recv.at[k, index(held)], sibling)

    def send_own(k, src, plane):
        own = block(k, (0, 0))
        for dy, dz in STRAIGHT:
            pltpu.make_async_remote_copy(
                src_ref=src, dst_ref=own, send_sem=seg_send.at[k], recv_sem=seg_recv.at[k, index((dy, dz))],
                device_id=(plane, ((y + dy) % Y * Z + (z + dz) % Z) * CORES + c), device_id_type=MESH,
            ).start()

    def pass_on(k, held):
        wait_bytes(block(k, held), seg_recv.at[k, index(held)])
        for offset in FAR_FIRST:
            if 0 not in offset:
                if (offset[0], 0) == held if abs(offset[1]) <= 2 else (0, offset[1]) == held:
                    ship(k, held, offset)
        to_sibling(k, held)

    def get_ready():
        for i in range(4):
            wait_bytes(mats.at[i // 2, i % 2], mat_sem.at[i])
        for k in range(1, layers):
            other = (r + k) % layers
            wait_bytes(prof_v.at[other], p_recv.at[other])
        for copy in profile_copies:
            copy.wait_send()
        to_scalar = pltpu.make_async_copy(prof_v, prof_s, p_local)
        to_scalar.start()
        to_scalar.wait()

    def multiply(k, kind, group, prof):
        first, end = group
        left = mats[ways[k], kind, prof, :, :, pl.ds(first * 128, (end - first) * 128)]
        right = [seg[k, ((y - dy) % Y) * Z + (z - dz) % Z].reshape(128, 128) for dy, dz in ORDER[first:end]]
        return jnp.dot(left.reshape(128, -1), jnp.concatenate(right, axis=0), preferred_element_type=F32)

    def collect(k):
        kinds = (0, 1) if k == 2 else (0,)
        totals = [jnp.zeros((128, 128), F32) for _ in kinds]
        if k == 2:
            @pl.when(outer)
            def _():
                wait_bytes(block(2, (0, 0)), seg_recv.at[2, 0])
                to_sibling(2, (0, 0))
        for n, held in enumerate(OFFSETS, 1):
            pass_on(k, held)
            if n == len(STRAIGHT) and k == 0:
                get_ready()
            if n in GROUPS:
                for offset in ORDER[slice(*GROUPS[n])]:
                    wait_bytes(sib_block(k, offset), sib_recv.at[k, index(offset)])
                prof = prof_s[layer_of[k], 0, 0]
                for t, kind in enumerate(kinds):
                    totals[t] += multiply(k, kind, GROUPS[n], prof)
        return [rotate_parts(total) for total in totals]

    def field(k):
        prof = prof_s[layer_of[k], 0, 0]
        return rotate_parts(sum(multiply(k, 1, group, prof) for group in GROUPS.values()))

    def to_layer(k, mine, send, theirs, recv):
        return pltpu.make_async_remote_copy(
            src_ref=mine.at[k], dst_ref=theirs.at[r], send_sem=send.at[k], recv_sem=recv.at[r],
            device_id=(layer_of[k], d), device_id_type=MESH,
        )

    trace_copies = [to_layer(k, my_trace, tr_send, traces, tr_recv) for k in range(3)]
    field_copies = [to_layer(k, my_field, mid_send, fields, mid_recv) for k in range(3)]

    force = find_force(0)
    seg[0, y * Z + z, c] = force
    pl.semaphore_wait(barrier, len(peers))
    send_own(0, block(0, (0, 0)), r)
    to_sibling(0, (0, 0))
    for copy in mat_copies:
        copy.start()
    forces[way_01] = force
    forces[1 - way_01] = find_force(1)
    for copy in profile_copies:
        copy.start()

    i_in = lax.broadcasted_iota(jnp.int32, (512, 512), 0)
    i_out = lax.broadcasted_iota(jnp.int32, (512, 512), 1)
    goal = ((i_in % 128) // 64) * 256 + 4 * (i_in % 64) + i_in // 128
    place[...] = jnp.where(i_out == goal, 1.0, 0.0).astype(BF16)
    fields[r] = jnp.zeros((64, 128), F32)

    across = pltpu.make_async_remote_copy(
        src_ref=my_trace.at[1], dst_ref=block(2, (0, 0)), send_sem=x_send, recv_sem=seg_recv.at[2, 0],
        device_id=(3 - r, d), device_id_type=MESH,
    )

    for k in range(3):
        results = collect(k)
        trace = results[0].astype(BF16)
        if k < 2:
            my_trace[k] = trace
        if k == 0:
            seg[1, y * Z + z, c] = jnp.where(middle, forces[1 - way_01], trace)
            send_own(1, block(1, (0, 0)), r)
            to_sibling(1, (0, 0))

            @pl.when(middle)
            def _():
                seg[2, y * Z + z, c] = trace
                send_own(2, block(2, (0, 0)), r)
                to_sibling(2, (0, 0))
        elif k == 1:
            @pl.when(outer)
            def _():
                send_own(2, my_trace.at[1], 3 - r)
                across.start()
        if k < 2:
            trace_copies[k].start()
            my_field[k] = field(k)
            field_copies[k].start()

    @pl.when(middle)
    def _():
        my_trace[2] = trace
        my_field[2] = results[1]
        trace_copies[2].start()
        field_copies[2].start()

    @pl.when(outer)
    def _():
        traces[3 - r] = trace
        fields[3 - r] = results[1]

    for k in range(1, layers):
        other = (r + k) % layers

        @pl.when(jnp.logical_or(middle, other != 3 - r))
        def _():
            wait_bytes(traces.at[other], tr_recv.at[other])
            wait_bytes(fields.at[other], mid_recv.at[other])
    traces[r] = forces[0]
    empty = jnp.zeros((64, 128), BF16)
    down = [jnp.where(i <= r, traces[i], empty) for i in range(layers)]
    traces[r] = forces[1]
    up = [jnp.where(i >= r, traces[i], empty) for i in range(layers)]
    both = jnp.concatenate([jnp.concatenate(down, axis=1), jnp.concatenate(up, axis=1)], axis=0)
    moved = jnp.dot(both, place[...], preferred_element_type=F32).astype(BF16)
    for part in range(2):
        down_out[0, part] = moved[:64, part * 256:(part + 1) * 256]
        up_out[0, part] = moved[64:, part * 256:(part + 1) * 256]

    whole = jnp.concatenate([fields[i] for i in range(layers)], axis=1)
    first = whole.astype(BF16)
    rest = whole - first.astype(F32)
    second = rest.astype(BF16)
    third = (rest - second.astype(F32)).astype(BF16)
    pieces = jnp.concatenate([first, second, third], axis=0)
    moved = jnp.dot(pieces, place[...], preferred_element_type=F32)
    moved = moved[0:64] + moved[64:128] + moved[128:192]
    for part in range(2):
        mid_out[0, part] = moved[:, part * 256:(part + 1) * 256]

    for k in range(3):
        wait_bytes(seg.at[:, pl.ds(0, 21), 0], seg_send.at[k])
    for k in range(2):
        trace_copies[k].wait_send()
        field_copies[k].wait_send()

    @pl.when(middle)
    def _():
        trace_copies[2].wait_send()
        field_copies[2].wait_send()

    @pl.when(outer)
    def _():
        across.wait_send()


def store(down, up, mid, down_out, up_out, mid_out, sem):
    copies = [
        pltpu.make_async_copy(src, dst, sem.at[i])
        for i, (src, dst) in enumerate(((mid, mid_out), (down, down_out), (up, up_out)))
    ]
    for copy in copies:
        copy.start()
    for copy in copies:
        copy.wait()


def body(
    transfer_down, transfer_up, field_from_top, field_from_bottom, source_to_bottom, source_to_top, profile, source_depth,
):
    hbm = pl.BlockSpec(memory_space=pl.ANY)
    vmem = pl.BlockSpec(memory_space=pltpu.VMEM)
    dma = pltpu.SemaphoreType.DMA
    outs = (
        jax.ShapeDtypeStruct((1, 2, 64, 256), BF16),
        jax.ShapeDtypeStruct((1, 2, 64, 256), BF16),
        jax.ShapeDtypeStruct((1, 2, 64, 256), F32),
    )
    results = pl.pallas_call(
        kernel,
        out_shape=tuple(pltpu.VMEM(o.shape, o.dtype) for o in outs),
        in_specs=[hbm] * 8,
        out_specs=(vmem, vmem, vmem),
        scratch_shapes=[
            pltpu.VMEM((2, 2, 2, 2, 64, 4096), BF16),
            *[pltpu.VMEM((2, 2, 64, HALF), BF16)] * 4,
            pltpu.VMEM((3, Y * Z, CORES, 64, 128), BF16),
            pltpu.VMEM((4, 64, 128), BF16),
            pltpu.VMEM((4, 64, 128), F32),
            pltpu.VMEM((2, 64, 128), BF16),
            pltpu.VMEM((3, 64, 128), BF16),
            pltpu.VMEM((3, 64, 128), F32),
            pltpu.VMEM((512, 512), BF16),
            pltpu.VMEM((4, 8, 128), jnp.int32),
            pltpu.SMEM((4, 8, 128), jnp.int32),
            pltpu.VMEM((4096, 128), BF16),
            pltpu.SMEM((1,), jnp.int32), pltpu.VMEM((1, 256), jnp.int32), dma((2,)),
            dma((4,)), dma((2, 2)),
            dma((3,)), dma((3, Y * Z)), dma((3, Y * Z)),
            dma((3,)), dma((4,)), dma((3,)), dma((4,)),
            dma((4,)), dma((4,)), dma(()),
            dma(()),
        ],
        compiler_params=pltpu.CompilerParams(
            collective_id=0, has_side_effects=True, vmem_limit_bytes=60 * 2**20
        ),
        cost_estimate=pl.CostEstimate(flops=10**9, bytes_accessed=13 * 2**20, transcendentals=0),
        name="sweeps",
    )(
        profile, source_depth.reshape(1, 256),
        transfer_down, transfer_up, field_from_top, field_from_bottom, source_to_bottom, source_to_top,
    )
    return pl.pallas_call(
        store,
        out_shape=outs,
        in_specs=[vmem] * 3,
        out_specs=(hbm,) * 3,
        scratch_shapes=[dma((3,))],
        name="store",
    )(*[pltpu.with_memory_space_constraint(x, pltpu.VMEM) for x in results])


def solution(mesh):
    rows = P(None, None, "depth", None)
    return jax.shard_map(
        body,
        mesh=mesh,
        in_specs=(rows,) * 6 + (P("range"), P()),
        out_specs=(P("range", None, "depth", None),) * 3,
        check_vma=False,
    )
```

```python
import functools

import jax
import jax.numpy as jnp
from jax import lax
from jax.experimental import pallas as pl
from jax.experimental.pallas import tpu as pltpu
from jax.sharding import PartitionSpec as P

MESH = pl.DeviceIdType.MESH
Y, Z, CORES = 4, 8, 2
FAR_FIRST = [(dy, dz) for dy in (0, 1, -1, 2) for dz in (0, 1, -1, 2, -2, 3, -3, 4) if (dy, dz) != (0, 0)]
FAR_FIRST.sort(key=lambda o: -abs(o[0]) - abs(o[1]))
STRAIGHT = [o for o in FAR_FIRST if 0 in o or abs(o[0]) == abs(o[1]) == 1]
OFFSETS = sorted(
    FAR_FIRST,
    key=lambda o: (0 not in o or 0 < abs(o[1]) <= 2, 0 not in o, o[1] != 0 and 0 in o, abs(o[0]) + abs(o[1])),
)
ORDER = [(0, 0)] + OFFSETS
GROUPS = {26: (0, 20), 31: (20, 32)}
CHUNK, HALF = 1024, 2048
BF16, F32 = jnp.bfloat16, jnp.float32


def wait_bytes(ref, sem):
    pltpu.make_async_copy(ref, ref, sem).wait()


def rotate_parts(product):
    rows, columns = product.shape[0] // 2, product.shape[1]
    swapped = pltpu.roll(product[rows:], columns // 2, 1)
    lane = lax.broadcasted_iota(jnp.int32, swapped.shape, 1)
    return product[:rows] + jnp.where(lane < columns // 2, -swapped, swapped)


def kernel(
    profile, depth, t_down, t_up, f_top, f_bottom, s_bottom, s_top,
    down_out, up_out, mid_out,
    mats, src_0, src_1, src_2, src_3, seg, traces, fields, forces, my_trace, my_field, place, prof_v, prof_s,
    hot, own_profile, depth_v, small_sem, mat_sem, src_sem, seg_send, seg_recv, sib_recv, tr_send, tr_recv, mid_send, mid_recv, p_send, p_recv, p_local, x_send,
):
    layers = 4
    srcs = (src_0, src_1, src_2, src_3)
    r = lax.axis_index("range")
    d = lax.axis_index("depth")
    y, z, c = d // (Z * CORES), (d // CORES) % Z, d % CORES

    def at(yy, zz, cc):
        return (r, ((yy % Y) * Z + zz % Z) * CORES + cc)

    sibling = at(y, z, 1 - c)

    barrier = pltpu.get_barrier_semaphore()
    peers = [at(y, z + k, c) for k in range(1, Z)] + [at(y + k, z, c) for k in range(1, Y)] + [sibling]
    peers += [at(y + i, z + j, c) for i in (1, -1) for j in (1, -1)]
    peers += [((r + k) % layers, d) for k in range(1, layers)]
    for peer in peers:
        pl.semaphore_signal(barrier, inc=1, device_id=peer, device_id_type=MESH)

    down_first = r < 2
    way_01 = jnp.where(down_first, 0, 1)

    src_copies = [
        [
            pltpu.make_async_copy(ref.at[:, :, :, pl.ds(half * HALF, HALF)], srcs[2 * i + half], src_sem.at[i, half])
            for i, ref in enumerate(refs) for half in range(2)
        ]
        for refs in ((s_bottom, s_top), (s_top, s_bottom))
    ]
    for way in range(2):
        @pl.when(way_01 == way)
        def _():
            for copy in src_copies[way]:
                copy.start()
    mat_copies = [
        pltpu.make_async_copy(
            ref.at[:, :, :, pl.ds(pl.multiple_of((((y - dy) % Y) * Z + (z - dz) % Z) * 128, 128), 128)],
            mats.at[i // 2, i % 2, :, :, :, pl.ds(place_in * 128, 128)],
            mat_sem.at[i],
        )
        for i, ref in enumerate((t_down, f_top, t_up, f_bottom)) for place_in, (dy, dz) in enumerate(ORDER)
    ]

    copies = [pltpu.make_async_copy(profile, own_profile, small_sem.at[0]), pltpu.make_async_copy(depth, depth_v, small_sem.at[1])]
    for copy in copies:
        copy.start()
    for copy in copies:
        copy.wait()
    my_profile = own_profile[0]
    prof_v[r] = jnp.full(prof_v.shape[1:], my_profile, jnp.int32)

    every = depth_v[...]
    pick_s = lax.broadcasted_iota(jnp.int32, (256, 128), 0)
    pick_j = lax.broadcasted_iota(jnp.int32, (256, 128), 1)
    pick = jnp.where(pick_s == 4 * (pick_j % 64) + r, 1.0, 0.0).astype(BF16)
    high = jnp.broadcast_to(every // 64, (16, 256)).astype(F32).astype(BF16)
    low = jnp.broadcast_to(every % 64, (16, 256)).astype(F32).astype(BF16)
    chosen = jnp.dot(high, pick, preferred_element_type=F32) * 64.0 + jnp.dot(low, pick, preferred_element_type=F32)
    chosen = chosen[0:1].astype(jnp.int32)

    for k0 in range(0, 4096, CHUNK):
        rows = lax.broadcasted_iota(jnp.int32, (CHUNK, 128), 0) + k0
        hot[pl.ds(k0, CHUNK)] = jnp.where(rows == chosen, 1.0, 0.0).astype(BF16)
    lane = lax.broadcasted_iota(jnp.int32, (64, 128), 1)

    def find_force(i):
        total = jnp.zeros((128, 128), F32)
        for half in range(2):
            src = srcs[2 * i + half]
            wait_bytes(src, src_sem.at[i, half])
            total += jnp.dot(
                src[my_profile].reshape(128, HALF), hot[pl.ds(half * HALF, HALF)], preferred_element_type=F32
            )
        return jnp.where(lane < 64, total[:64], total[64:]).astype(BF16)

    middle = jnp.logical_or(r == 1, r == 2)
    outer = jnp.logical_not(middle)
    ways = (way_01, r % 2, 1 - r % 2)
    layer_of = (1 + r % 2, jnp.where(r == 0, 2, jnp.where(r == 1, 0, jnp.where(r == 2, 3, 1))), 3 * (r % 2))

    profile_copies = [
        pltpu.make_async_remote_copy(
            src_ref=prof_v.at[r], dst_ref=prof_v.at[r], send_sem=p_send.at[k], recv_sem=p_recv.at[r],
            device_id=((r + k) % layers, d), device_id_type=MESH,
        )
        for k in range(1, layers)
    ]

    def block(k, offset):
        return seg.at[k, ((y - offset[0]) % Y) * Z + (z - offset[1]) % Z, c]

    def sib_block(k, offset):
        return seg.at[k, ((y - offset[0]) % Y) * Z + (z - offset[1]) % Z, 1 - c]

    def index(offset):
        return (offset[0] % Y) * Z + offset[1] % Z

    def put(ref, send, recv, to):
        pltpu.make_async_remote_copy(
            src_ref=ref, dst_ref=ref, send_sem=send, recv_sem=recv, device_id=to, device_id_type=MESH
        ).start()

    def ship(k, held, offset):
        put(
            block(k, held), seg_send.at[k], seg_recv.at[k, index(offset)],
            at(y + offset[0] - held[0], z + offset[1] - held[1], c),
        )

    def to_sibling(k, held):
        put(block(k, held), seg_send.at[k], sib_recv.at[k, index(held)], sibling)

    def send_own(k, src, plane):
        own = block(k, (0, 0))
        for dy, dz in STRAIGHT:
            pltpu.make_async_remote_copy(
                src_ref=src, dst_ref=own, send_sem=seg_send.at[k], recv_sem=seg_recv.at[k, index((dy, dz))],
                device_id=(plane, ((y + dy) % Y * Z + (z + dz) % Z) * CORES + c), device_id_type=MESH,
            ).start()

    def pass_on(k, held):
        wait_bytes(block(k, held), seg_recv.at[k, index(held)])
        for offset in FAR_FIRST:
            if offset not in STRAIGHT:
                if (offset[0], 0) == held if abs(offset[1]) <= 2 else (0, offset[1]) == held:
                    ship(k, held, offset)
        to_sibling(k, held)

    def get_ready():
        for i in range(4):
            wait_bytes(mats.at[i // 2, i % 2], mat_sem.at[i])
        for k in range(1, layers):
            other = (r + k) % layers
            wait_bytes(prof_v.at[other], p_recv.at[other])
        for copy in profile_copies:
            copy.wait_send()
        to_scalar = pltpu.make_async_copy(prof_v, prof_s, p_local)
        to_scalar.start()
        to_scalar.wait()

    def multiply(k, kind, group, prof):
        first, end = group
        left = mats[ways[k], kind, prof, :, :, pl.ds(first * 128, (end - first) * 128)]
        right = [seg[k, ((y - dy) % Y) * Z + (z - dz) % Z].reshape(128, 128) for dy, dz in ORDER[first:end]]
        return jnp.dot(left.reshape(128, -1), jnp.concatenate(right, axis=0), preferred_element_type=F32)

    def collect(k):
        kinds = (0, 1) if k == 2 else (0,)
        totals = [jnp.zeros((128, 128), F32) for _ in kinds]
        if k == 2:
            @pl.when(outer)
            def _():
                wait_bytes(block(2, (0, 0)), seg_recv.at[2, 0])
                to_sibling(2, (0, 0))
        for n, held in enumerate(OFFSETS, 1):
            pass_on(k, held)
            if n == len(STRAIGHT) and k == 0:
                get_ready()
            if n in GROUPS:
                for offset in ORDER[slice(*GROUPS[n])]:
                    wait_bytes(sib_block(k, offset), sib_recv.at[k, index(offset)])
                prof = prof_s[layer_of[k], 0, 0]
                for t, kind in enumerate(kinds):
                    totals[t] += multiply(k, kind, GROUPS[n], prof)
        return [rotate_parts(total) for total in totals]

    def field(k):
        prof = prof_s[layer_of[k], 0, 0]
        return rotate_parts(sum(multiply(k, 1, group, prof) for group in GROUPS.values()))

    def to_layer(k, mine, send, theirs, recv):
        return pltpu.make_async_remote_copy(
            src_ref=mine.at[k], dst_ref=theirs.at[r], send_sem=send.at[k], recv_sem=recv.at[r],
            device_id=(layer_of[k], d), device_id_type=MESH,
        )

    trace_copies = [to_layer(k, my_trace, tr_send, traces, tr_recv) for k in range(3)]
    field_copies = [to_layer(k, my_field, mid_send, fields, mid_recv) for k in range(3)]

    force = find_force(0)
    seg[0, y * Z + z, c] = force
    pl.semaphore_wait(barrier, len(peers))
    send_own(0, block(0, (0, 0)), r)
    to_sibling(0, (0, 0))
    for copy in mat_copies:
        copy.start()
    forces[way_01] = force
    forces[1 - way_01] = find_force(1)
    for copy in profile_copies:
        copy.start()

    i_in = lax.broadcasted_iota(jnp.int32, (512, 512), 0)
    i_out = lax.broadcasted_iota(jnp.int32, (512, 512), 1)
    goal = ((i_in % 128) // 64) * 256 + 4 * (i_in % 64) + i_in // 128
    place[...] = jnp.where(i_out == goal, 1.0, 0.0).astype(BF16)
    fields[r] = jnp.zeros((64, 128), F32)

    across = pltpu.make_async_remote_copy(
        src_ref=my_trace.at[1], dst_ref=block(2, (0, 0)), send_sem=x_send, recv_sem=seg_recv.at[2, 0],
        device_id=(3 - r, d), device_id_type=MESH,
    )

    for k in range(3):
        results = collect(k)
        trace = results[0].astype(BF16)
        if k < 2:
            my_trace[k] = trace
        if k == 0:
            seg[1, y * Z + z, c] = jnp.where(middle, forces[1 - way_01], trace)
            send_own(1, block(1, (0, 0)), r)
            to_sibling(1, (0, 0))

            @pl.when(middle)
            def _():
                seg[2, y * Z + z, c] = trace
                send_own(2, block(2, (0, 0)), r)
                to_sibling(2, (0, 0))
        elif k == 1:
            @pl.when(outer)
            def _():
                send_own(2, my_trace.at[1], 3 - r)
                across.start()
        if k < 2:
            trace_copies[k].start()
            my_field[k] = field(k)
            field_copies[k].start()

    @pl.when(middle)
    def _():
        my_trace[2] = trace
        my_field[2] = results[1]
        trace_copies[2].start()
        field_copies[2].start()

    @pl.when(outer)
    def _():
        traces[3 - r] = trace
        fields[3 - r] = results[1]

    for k in range(1, layers):
        other = (r + k) % layers

        @pl.when(jnp.logical_or(middle, other != 3 - r))
        def _():
            wait_bytes(traces.at[other], tr_recv.at[other])
            wait_bytes(fields.at[other], mid_recv.at[other])
    traces[r] = forces[0]
    empty = jnp.zeros((64, 128), BF16)
    down = [jnp.where(i <= r, traces[i], empty) for i in range(layers)]
    traces[r] = forces[1]
    up = [jnp.where(i >= r, traces[i], empty) for i in range(layers)]
    both = jnp.concatenate([jnp.concatenate(down, axis=1), jnp.concatenate(up, axis=1)], axis=0)
    moved = jnp.dot(both, place[...], preferred_element_type=F32).astype(BF16)
    for part in range(2):
        down_out[0, part] = moved[:64, part * 256:(part + 1) * 256]
        up_out[0, part] = moved[64:, part * 256:(part + 1) * 256]

    whole = jnp.concatenate([fields[i] for i in range(layers)], axis=1)
    first = whole.astype(BF16)
    rest = whole - first.astype(F32)
    second = rest.astype(BF16)
    third = (rest - second.astype(F32)).astype(BF16)
    pieces = jnp.concatenate([first, second, third], axis=0)
    moved = jnp.dot(pieces, place[...], preferred_element_type=F32)
    moved = moved[0:64] + moved[64:128] + moved[128:192]
    for part in range(2):
        mid_out[0, part] = moved[:, part * 256:(part + 1) * 256]

    for k in range(3):
        wait_bytes(seg.at[:, pl.ds(0, 21), 0], seg_send.at[k])
    for k in range(2):
        trace_copies[k].wait_send()
        field_copies[k].wait_send()

    @pl.when(middle)
    def _():
        trace_copies[2].wait_send()
        field_copies[2].wait_send()

    @pl.when(outer)
    def _():
        across.wait_send()


def store(down, up, mid, down_out, up_out, mid_out, sem):
    copies = [
        pltpu.make_async_copy(src, dst, sem.at[i])
        for i, (src, dst) in enumerate(((mid, mid_out), (down, down_out), (up, up_out)))
    ]
    for copy in copies:
        copy.start()
    for copy in copies:
        copy.wait()


def body(
    transfer_down, transfer_up, field_from_top, field_from_bottom, source_to_bottom, source_to_top, profile, source_depth,
):
    hbm = pl.BlockSpec(memory_space=pl.ANY)
    vmem = pl.BlockSpec(memory_space=pltpu.VMEM)
    dma = pltpu.SemaphoreType.DMA
    outs = (
        jax.ShapeDtypeStruct((1, 2, 64, 256), BF16),
        jax.ShapeDtypeStruct((1, 2, 64, 256), BF16),
        jax.ShapeDtypeStruct((1, 2, 64, 256), F32),
    )
    results = pl.pallas_call(
        kernel,
        out_shape=tuple(pltpu.VMEM(o.shape, o.dtype) for o in outs),
        in_specs=[vmem] + [hbm] * 7,
        out_specs=(vmem, vmem, vmem),
        scratch_shapes=[
            pltpu.VMEM((2, 2, 2, 2, 64, 4096), BF16),
            *[pltpu.VMEM((2, 2, 64, HALF), BF16)] * 4,
            pltpu.VMEM((3, Y * Z, CORES, 64, 128), BF16),
            pltpu.VMEM((4, 64, 128), BF16),
            pltpu.VMEM((4, 64, 128), F32),
            pltpu.VMEM((2, 64, 128), BF16),
            pltpu.VMEM((3, 64, 128), BF16),
            pltpu.VMEM((3, 64, 128), F32),
            pltpu.VMEM((512, 512), BF16),
            pltpu.VMEM((4, 8, 128), jnp.int32),
            pltpu.SMEM((4, 8, 128), jnp.int32),
            pltpu.VMEM((4096, 128), BF16),
            pltpu.SMEM((1,), jnp.int32), pltpu.VMEM((1, 256), jnp.int32), dma((2,)),
            dma((4,)), dma((2, 2)),
            dma((3,)), dma((3, Y * Z)), dma((3, Y * Z)),
            dma((3,)), dma((4,)), dma((3,)), dma((4,)),
            dma((4,)), dma((4,)), dma(()),
            dma(()),
        ],
        compiler_params=pltpu.CompilerParams(
            collective_id=0, has_side_effects=True, vmem_limit_bytes=60 * 2**20
        ),
        cost_estimate=pl.CostEstimate(flops=10**9, bytes_accessed=13 * 2**20, transcendentals=0),
        name="sweeps",
    )(
        profile, source_depth.reshape(1, 256),
        transfer_down, transfer_up, field_from_top, field_from_bottom, source_to_bottom, source_to_top,
    )
    return pl.pallas_call(
        store,
        out_shape=outs,
        in_specs=[vmem] * 3,
        out_specs=(hbm,) * 3,
        scratch_shapes=[dma((3,))],
        name="store",
    )(*[pltpu.with_memory_space_constraint(x, pltpu.VMEM) for x in results])


def solution(mesh):
    rows = P(None, None, "depth", None)
    return jax.shard_map(
        body,
        mesh=mesh,
        in_specs=(rows,) * 6 + (P("range"), P()),
        out_specs=(P("range", None, "depth", None),) * 3,
        check_vma=False,
    )
```
